32 devices in a mesh: groups: 2 (over y), expert: 4 (over x, core), tensor: 4 (over z).
Axes of the slice: x: 2, y: 2, z: 4, core: 2. Of those that a mesh axis runs over, the one named last changes fastest.
Arguments:
- tokens: bfloat16 [1024, 6144], P(('groups', 'expert'), 'tensor'), parts along dimension 0, may hold values from -6 to 6
- routes: int32 [1024, 2], P(('groups', 'expert')), parts along dimension 0, may hold values from 0 to 3, all different within a row; in each aligned block of 128 rows (0 to 127, 128 to 255, ...) at most 72 rows name the same one
- route_weights: bfloat16 [1024, 2], P(('groups', 'expert')), parts along dimension 0, may hold values from 0.099609375 to 1
- gate_weight: bfloat16 [6144, 32768], P(None, ('expert', 'tensor')), may hold values from -0.078125 to 0.078125
- up_weight: bfloat16 [6144, 32768], P(None, ('expert', 'tensor')), may hold values from -0.078125 to 0.078125
- down_weight: bfloat16 [32768, 6144], P(('expert', 'tensor')), may hold values from -0.0625 to 0.0625
Outputs:
- mixed: bfloat16 [1024, 6144], P(('groups', 'expert'), 'tensor'), parts along dimension 0
The draws below stay inside these ranges and needn't reach their ends.
There are 2 independent parts, one for each index of `groups`. The reference program is written for one: setup_inputs(seed, part) draws one part's arguments, and reference() takes and returns one part's arrays. A program takes and returns all parts, laid end to end along the dimension named above; an argument that names none is the same for every part. Nothing has to cross between parts.
Inputs may be any that keep to these rules, and one draw needn't show every extreme that they name: `routes`: each row names 2 different experts. In each aligned block of 128 rows (the tokens of one index of the expert axis) no expert is named by more than 72 rows, a bound that some block reaches.
All inputs are finite; a program needn't handle non-finite values.
Results may differ from the reference program's by a relative error of at most 0.013.
Values may be sent and summed in bfloat16 or wider, within the bound.
A program may use at most 192 MiB of HBM per device.

```python
import math
import jax
import jax.numpy as jnp
import numpy as np
from jax import lax

D = 6144
EXPERTS = 4
FF = 8192
TOP = 2
TOK_DEV = 128
TOKENS = 512
CAP = 72
REPL = 1
FF_BLK = 2048
N_TENSOR = 4


def steps_of(rng, extent, cuts, smallest, largest):
    loudness = 1.0
    for position, parts in cuts:
        steps = jax.random.uniform(jax.random.fold_in(jax.random.fold_in(rng, 6), position), (parts,), jnp.float32, smallest / len(cuts), largest / len(cuts))
        loudness = loudness * jnp.repeat(jnp.exp(steps), extent[position] // parts).reshape((-1,) + (1,) * (len(extent) - 1 - position))
    return loudness


def routed_block(rng, own, number, rows, number_of, top, reach, lean):
    ranking = jax.random.permutation(rng, number_of)
    heavy_load, common = portions_of(number_of, rows * top, reach, lean, True), portions_of(number_of, rows * top, reach, lean, False)
    places = jnp.arange(number_of)

    def named(sizes, offset_by):
        used = int((sizes > 0).sum())
        fixed = max(1, used // 4)
        shifted = fixed + (places - fixed + offset_by * (used - fixed)) % max(1, number_of - fixed)
        return jnp.zeros((number_of,), jnp.int32).at[ranking[jnp.where(places < fixed, places, shifted)]].set(jnp.asarray(sizes, jnp.int32))

    sizes = jnp.where(number % 4 == 0, named(heavy_load, number // 4), named(common, number - number // 4 - 1))
    mixed = jax.random.permutation(jax.random.fold_in(own, 3), number_of)
    donor, taker = mixed[0:number_of // 2 * 2:2], mixed[1:number_of // 2 * 2:2]
    room = jnp.minimum(sizes[donor] - 1, reach - sizes[taker]) // 2
    room = jnp.where((donor == ranking[0]) | (taker == ranking[0]) | (sizes[taker] == 0), 0, jnp.maximum(room, 0))
    shifted = jax.random.randint(jax.random.fold_in(own, 4), (number_of // 2,), 0, 1 << 20) % (room + 1)
    sizes = sizes.at[donor].add(-shifted).at[taker].add(shifted)
    items = jnp.searchsorted(jnp.cumsum(sizes), jnp.arange(rows * top), side="right").astype(jnp.int32)
    grid = items.reshape(top, rows).T
    grid = grid[jax.random.permutation(jax.random.fold_in(own, 1), rows)]
    offset_by = jax.random.randint(jax.random.fold_in(own, 2), (rows, 1), 0, top)
    return jnp.take_along_axis(grid, (jnp.arange(top)[None, :] + offset_by) % top, axis=1)


def portions_of(amount, total, bound, lean, full):
    portions = [(1 << 20) // math.isqrt(rank ** lean) + 1 for rank in range(1, amount + 1)]
    largest = bound if full else min(bound, max(-(-total // amount), total * portions[0] // sum(portions)))
    least = 1 if total - largest >= amount - 1 else 0
    counts, rest = [largest] + [least] * (amount - 1), total - largest - least * (amount - 1)
    while rest > 0:
        free = [i for i in range(1, amount) if counts[i] < largest] or [i for i in range(1, amount) if counts[i] < bound]
        whole, left = sum([portions[i] for i in free]), rest
        for i in free:
            more = min(bound - counts[i], max(1, left * portions[i] // whole), rest)
            counts[i] = counts[i] + more
            rest = rest - more
    return np.array(counts)


def centred(key, dims, deviation, bound, cuts=(), kind=jnp.bfloat16):
    values = jax.random.normal(key, dims, jnp.float32) * deviation
    if len(cuts) > 0:
        values = steps_of(key, dims, cuts, -0.22, 0.18) * values
    return jnp.clip(values, min=-bound, max=bound).astype(kind)


def setup_inputs(seed: int = 0, part: int = 0) -> dict:
    streams_of = jax.random.split(jax.random.key(seed), 7)
    part_keys = jax.random.split(jax.random.fold_in(streams_of[6], part), 7)
    tokens = centred(part_keys[0], (TOKENS, D), 1.0, 6.0, ((0, 4), (1, 4)))
    routes_keys = jax.random.split(jax.random.fold_in(part_keys[1], 1), TOKENS // TOK_DEV)
    routes_turns = jax.random.permutation(jax.random.fold_in(part_keys[1], 3), TOKENS // TOK_DEV)
    routes = jax.vmap(lambda own, number: routed_block(jax.random.fold_in(part_keys[1], 2), own, number, TOK_DEV, EXPERTS, TOP, CAP, 2))(routes_keys, routes_turns).reshape((TOKENS, TOP))
    route_weights = jnp.clip(0.099609375 + 0.9003906 * jax.random.uniform(part_keys[2], (TOKENS, TOP), jnp.float32) ** steps_of(part_keys[2], (TOKENS, TOP), ((0, 4),), -0.2, 0.2), 0.099609375, 1.0).astype(jnp.bfloat16)
    gate_weight = centred(streams_of[3], (D, EXPERTS * FF), D ** -0.5, 0.078125, ((1, 16),))
    up_weight = centred(streams_of[4], (D, EXPERTS * FF), D ** -0.5, 0.078125, ((1, 16),))
    down_weight = centred(streams_of[5], (EXPERTS * FF, D), FF ** -0.5, 0.0625, ((0, 16),))
    return {"tokens": tokens, "routes": routes, "route_weights": route_weights, "gate_weight": gate_weight, "up_weight": up_weight, "down_weight": down_weight}


def reference(tokens, routes, route_weights, gate_weight, up_weight, down_weight):
    blocks = REPL * N_TENSOR
    weights = route_weights.astype(jnp.float32)
    mixed = jnp.zeros((TOKENS, D), jnp.float32)
    for expert in range(EXPERTS):
        low = expert * FF
        gate = jnp.dot(tokens, gate_weight[:, low:low + FF], preferred_element_type=jnp.float32)
        up = jnp.dot(tokens, up_weight[:, low:low + FF], preferred_element_type=jnp.float32)
        hidden = (jax.nn.silu(gate) * up).astype(jnp.bfloat16)
        pieces = hidden.reshape(TOKENS, blocks, FF_BLK).transpose(1, 0, 2)
        columns = down_weight[low:low + FF].reshape(blocks, FF_BLK, D)

        def add_block(total, pair):
            term = jnp.dot(pair[0], pair[1], preferred_element_type=jnp.float32).astype(jnp.bfloat16)
            term = lax.optimization_barrier(term)
            return total + term.astype(jnp.float32), None

        output, _ = lax.scan(add_block, jnp.zeros((TOKENS, D), jnp.float32), (pieces, columns))
        share = jnp.sum(jnp.where(routes == expert, weights, jnp.zeros_like(weights)), axis=1)
        mixed = mixed + share[:, None] * output
    return mixed.astype(jnp.bfloat16)
```

```python
import functools

import jax
import jax.numpy as jnp
from jax import lax
from jax.experimental import pallas as pl
from jax.experimental.pallas import tpu as pltpu
from jax.sharding import PartitionSpec as P

EXPERTS = 4
TOP = 2
CAP = 72
BF = jnp.bfloat16
F32 = jnp.float32
W_SLOTS = 3
D_SLOTS = 3
K_SLOTS = 4
ROLES = 4


def kernel(
    nt, nq, tok, meta, wg, wu, wd, out,
    xbuf, packed, acc_g, acc_u, hid, gbuf, ubuf, dbuf, pick, spread, meta_in,
    keep, sib_out, sib_in, x_out, x_in, z_out, z_in,
    tok_sem, w_sem, d_sem, meta_s, meta_r,
    zs_s, zs_r, xs_s, xs_r, own_s, own_r, fwd_s, fwd_r,
    rsib_s, rsib_r, rx_s, rx_r, rz_s, rz_r,
):
    n = nt * nq
    kc = xbuf.shape[3]
    tokens = tok.shape[0]
    rows = ROLES * CAP
    z = lax.axis_index("tensor")
    ex = lax.axis_index("expert")
    core = lax.rem(ex, 2)
    chip = lax.div(ex, 2)
    sib = 2 * chip + 1 - core
    xp = 2 * (1 - chip) + core
    dg = 2 * (1 - chip) + 1 - core
    my_expert = ex

    def offset(d):
        return lax.rem(z + ((d + 1) // 2) * (2 * (d % 2) - 1) + nt, nt)

    def offset_t(d):
        return lax.rem(z + lax.div(d + 1, 2) * (2 * lax.rem(d, 2) - 1) + nt, nt)

    def at_expert(src, dst, s, r, who):
        return pltpu.make_async_remote_copy(
            src_ref=src, dst_ref=dst, send_sem=s, recv_sem=r,
            device_id={"expert": who}, device_id_type=pl.DeviceIdType.MESH)

    def at_tensor(src, dst, s, r, who):
        return pltpu.make_async_remote_copy(
            src_ref=src, dst_ref=dst, send_sem=s, recv_sem=r,
            device_id={"tensor": who}, device_id_type=pl.DeviceIdType.MESH)

    def tok_copy(q):
        return pltpu.make_async_copy(
            tok.at[:, pl.ds(q * kc, kc)], xbuf.at[z * nq + q, 0], tok_sem.at[q])

    def g_copy(i, k):
        s = lax.rem(i, W_SLOTS)
        r = pl.ds(pl.multiple_of(k * kc, kc), kc)
        return pltpu.make_async_copy(wg.at[r, :], gbuf.at[s], w_sem.at[0, s])

    def u_copy(i, k):
        s = lax.rem(i, W_SLOTS)
        r = pl.ds(pl.multiple_of(k * kc, kc), kc)
        return pltpu.make_async_copy(wu.at[r, :], ubuf.at[s], w_sem.at[1, s])

    def d_copy(i, k):
        s = lax.rem(i, D_SLOTS)
        r = pl.ds(pl.multiple_of(k * kc, kc), kc)
        return pltpu.make_async_copy(wd.at[:, r], dbuf.at[s], d_sem.at[s])

    def in_chunk(i):
        return offset_t(lax.rem(i, nt)) * nq + lax.div(i, nt)

    def out_owner(i):
        return offset_t(lax.rem(i + 1, nt))

    def out_chunk(i):
        return out_owner(i) * nq + lax.div(i, nt)

    def z_copy(d, q):
        s = (d - 1) * nq + q
        k = z * nq + q
        return at_tensor(xbuf.at[k, 0], xbuf.at[k, 0], zs_s.at[s], zs_r.at[k], offset(d))

    def z_arrival(k):
        return at_tensor(xbuf.at[k, 0], xbuf.at[k, 0], zs_s.at[0], zs_r.at[k], offset(1))

    def x_copy(k):
        return at_expert(xbuf.at[k, 0], xbuf.at[k, 1], xs_s.at[k], xs_r.at[k], xp)

    def own_copy(k):
        return at_expert(xbuf.at[k, 0], xbuf.at[k, 2], own_s.at[k], own_r.at[k], sib)

    def fwd_copy(k):
        return at_expert(xbuf.at[k, 1], xbuf.at[k, 3], fwd_s.at[k], fwd_r.at[k], sib)

    def rsib_copy(k):
        return at_expert(sib_out.at[k], sib_in.at[k], rsib_s.at[k], rsib_r.at[k], sib)

    def rx_copy(k):
        return at_expert(x_out.at[k], x_in.at[k], rx_s.at[k], rx_r.at[k], xp)

    def rz_copy(k, q, who):
        return at_tensor(z_out.at[k], z_in.at[z * nq + q], rz_s.at[k], rz_r.at[z * nq + q], who)

    def rz_arrival(k):
        return at_tensor(z_out.at[k], z_in.at[k], rz_s.at[k], rz_r.at[k], offset(1))

    def meta_copy(role, who):
        return at_expert(
            meta.at[who], meta_in.at[role], meta_s.at[role], meta_r.at[role], who)

    for q in range(nq):
        tok_copy(q).start()
    for i in range(W_SLOTS):
        g_copy(i, in_chunk(i)).start()
        u_copy(i, in_chunk(i)).start()

    barrier = pltpu.get_barrier_semaphore()
    for who in (sib, xp, dg):
        pl.semaphore_signal(
            barrier, inc=1, device_id={"expert": who}, device_id_type=pl.DeviceIdType.MESH)
    for d in range(1, nt):
        pl.semaphore_signal(
            barrier, inc=1, device_id={"tensor": offset(d)}, device_id_type=pl.DeviceIdType.MESH)
    pl.semaphore_wait(barrier, 3 + nt - 1)

    partners = ((1, xp), (2, sib), (3, dg))
    for role, who in partners:
        meta_copy(role, who).start()
    for q in range(nq):
        tok_copy(q).wait()
        for d in range(1, nt):
            z_copy(d, q).start()
        x_copy(z * nq + q).start()
        own_copy(z * nq + q).start()
    for i in range(D_SLOTS):
        d_copy(i, out_chunk(i)).start()

    acc_g[...] = jnp.zeros_like(acc_g)
    acc_u[...] = jnp.zeros_like(acc_u)
    meta_in[0] = meta[my_expert]
    for role, who in partners:
        meta_copy(role, who).wait_recv()
    eye = lax.broadcasted_iota(jnp.int32, (tokens, tokens), 0) == lax.broadcasted_iota(
        jnp.int32, (tokens, tokens), 1)
    row_id = lax.broadcasted_iota(jnp.int32, (rows, tokens), 0).astype(F32)
    for role in range(ROLES):
        slot = meta_in[role, 0:1, :]
        weight = meta_in[role, 1:2, :]
        slot = jnp.where(slot >= 0, slot + role * CAP, -1.0)
        hot = jnp.where(row_id == slot, 1.0, 0.0).astype(BF)
        pick[:, role * tokens:(role + 1) * tokens] = hot
        scale = jnp.where(eye, jnp.broadcast_to(weight, (tokens, tokens)), 0.0).astype(BF)
        spread[role * tokens:(role + 1) * tokens, :] = lax.dot_general(
            scale, hot, (((1,), (1,)), ((), ())), preferred_element_type=F32).astype(BF)

    tile = 512 if gbuf.shape[2] % 512 == 0 else gbuf.shape[2]

    def gather_step(i, carry):
        @pl.when(i < n)
        def _():
            @pl.when(lax.rem(i, nt) > 0)
            def _():
                k = in_chunk(i)
                z_arrival(k).wait_recv()
                x_copy(k).start()
                own_copy(k).start()

        @pl.when((i >= 1) & (i < n + 1))
        def _():
            k = in_chunk(i - 1)
            x_copy(k).wait_recv()
            fwd_copy(k).start()

        @pl.when(i >= 2)
        def _():
            j = i - 2
            k = in_chunk(j)
            s = lax.rem(j, W_SLOTS)
            own_copy(k).wait_recv()
            fwd_copy(k).wait_recv()
            packed[...] = jnp.dot(
                pick[...], xbuf[k].reshape(ROLES * tokens, kc), preferred_element_type=F32
            ).astype(BF)
            g_copy(j, k).wait()
            u_copy(j, k).wait()

            def column(t, c2):
                cols = pl.ds(pl.multiple_of(t * tile, tile), tile)
                acc_g[:, cols] += jnp.dot(packed[...], gbuf[s, :, cols], preferred_element_type=F32)
                acc_u[:, cols] += jnp.dot(packed[...], ubuf[s, :, cols], preferred_element_type=F32)
                return c2

            lax.fori_loop(0, gbuf.shape[2] // tile, column, 0)

            @pl.when(j + W_SLOTS < n)
            def _():
                k2 = in_chunk(j + W_SLOTS)
                g_copy(j + W_SLOTS, k2).start()
                u_copy(j + W_SLOTS, k2).start()

        return carry

    lax.fori_loop(0, n + 2, gather_step, 0)

    def activate(t, carry):
        cols = pl.ds(pl.multiple_of(t * tile, tile), tile)
        hid[:, cols] = (jax.nn.silu(acc_g[:, cols]) * acc_u[:, cols]).astype(BF)
        return carry

    lax.fori_loop(0, gbuf.shape[2] // tile, activate, 0)

    width = 256

    def return_step(i, carry):
        @pl.when(i < n)
        def _():
            k = out_chunk(i)
            s = lax.rem(i, D_SLOTS)
            ks = lax.rem(i, K_SLOTS)
            d_copy(i, k).wait()

            def column(t, c2):
                cols = pl.ds(pl.multiple_of(t * width, width), width)
                term = jnp.dot(hid[...], dbuf[s, :, cols], preferred_element_type=F32).astype(BF)
                share = jnp.dot(spread[...], term, preferred_element_type=F32)
                keep[ks, :, cols] = share[:2 * tokens]
                sib_out[k, :, cols] = share[2 * tokens:].astype(BF)
                return c2

            lax.fori_loop(0, kc // width, column, 0)
            rsib_copy(k).start()

            @pl.when(i + D_SLOTS < n)
            def _():
                d_copy(i + D_SLOTS, out_chunk(i + D_SLOTS)).start()

        @pl.when((i >= 1) & (i < n + 1))
        def _():
            k = out_chunk(i - 1)
            ks = lax.rem(i - 1, K_SLOTS)
            rsib_copy(k).wait_recv()
            x_out[k] = (keep[ks, tokens:] + sib_in[k, tokens:].astype(F32)).astype(BF)
            rx_copy(k).start()

        @pl.when(i >= 2)
        def _():
            j = i - 2
            k = out_chunk(j)
            ks = lax.rem(j, K_SLOTS)
            rx_copy(k).wait_recv()
            z_out[k] = (
                keep[ks, :tokens] + sib_in[k, :tokens].astype(F32) + x_in[k].astype(F32)
            ).astype(BF)

            @pl.when(lax.rem(j + 1, nt) > 0)
            def _():
                rz_copy(k, lax.div(j, nt), out_owner(j)).start()

        return carry

    lax.fori_loop(0, n + 2, return_step, 0)

    for q in range(nq):
        total = z_out[z * nq + q].astype(F32)
        for d in range(1, nt):
            k = offset(d) * nq + q
            rz_arrival(k).wait_recv()
            total = total + z_in[k].astype(F32)
        out[:, q * kc:(q + 1) * kc] = total.astype(BF)

    for role, who in partners:
        meta_copy(role, who).wait_send()
    for q in range(nq):
        for d in range(1, nt):
            z_copy(d, q).wait_send()

    def drain(k, carry):
        x_copy(k).wait_send()
        own_copy(k).wait_send()
        fwd_copy(k).wait_send()
        rsib_copy(k).wait_send()
        rx_copy(k).wait_send()
        return carry

    lax.fori_loop(0, n, drain, 0)
    for q in range(nq):
        for d in range(1, nt):
            rz_copy(offset(d) * nq + q, q, offset(d)).wait_send()


def fused(mesh, tokens, routes, route_weights, gate_weight, up_weight, down_weight):
    nt = mesh.shape["tensor"]
    count, local_width = tokens.shape
    hidden = gate_weight.shape[1]
    kc = 768
    nq = local_width // kc
    n = nt * nq
    rows = ROLES * CAP
    ids = lax.broadcasted_iota(jnp.int32, (EXPERTS, 1, 1), 0)
    named = routes.T[None] == ids
    hit = named.any(axis=1)
    share = jnp.where(named, route_weights.T.astype(F32)[None], 0.0).sum(axis=1)
    before = (
        lax.broadcasted_iota(jnp.int32, (count, count), 0)
        < lax.broadcasted_iota(jnp.int32, (count, count), 1)
    )
    rank = jnp.dot(hit.astype(BF), before.astype(BF), preferred_element_type=F32)
    slot = jnp.where(hit, rank, -1.0)
    meta = jnp.concatenate(
        [slot[:, None], share[:, None], jnp.zeros((EXPERTS, 6, count), F32)], axis=1)
    dma = pltpu.SemaphoreType.DMA
    vmem = pltpu.VMEM
    any_spec = pl.BlockSpec(memory_space=pl.ANY)
    vmem_spec = pl.BlockSpec(memory_space=pltpu.VMEM)
    return pl.pallas_call(
        functools.partial(kernel, nt, nq),
        out_shape=jax.ShapeDtypeStruct((count, local_width), BF),
        in_specs=[any_spec, vmem_spec, any_spec, any_spec, any_spec],
        out_specs=vmem_spec,
        scratch_shapes=[
            vmem((n, ROLES, count, kc), BF),
            vmem((rows, kc), BF),
            vmem((rows, hidden), F32),
            vmem((rows, hidden), F32),
            vmem((rows, hidden), BF),
            vmem((W_SLOTS, kc, hidden), BF),
            vmem((W_SLOTS, kc, hidden), BF),
            vmem((D_SLOTS, hidden, kc), BF),
            vmem((rows, ROLES * count), BF),
            vmem((ROLES * count, rows), BF),
            vmem((ROLES, 8, count), F32),
            vmem((K_SLOTS, 2 * count, kc), F32),
            vmem((n, 2 * count, kc), BF),
            vmem((n, 2 * count, kc), BF),
            vmem((n, count, kc), BF),
            vmem((n, count, kc), BF),
            vmem((n, count, kc), BF),
            vmem((n, count, kc), BF),
            dma((nq,)), dma((2, W_SLOTS)), dma((D_SLOTS,)), dma((ROLES,)), dma((ROLES,)),
            dma(((nt - 1) * nq,)), dma((n,)), dma((n,)), dma((n,)), dma((n,)), dma((n,)),
            dma((n,)), dma((n,)), dma((n,)), dma((n,)), dma((n,)), dma((n,)), dma((n,)), dma((n,)),
        ],
        compiler_params=pltpu.CompilerParams(
            collective_id=0, has_side_effects=True, vmem_limit_bytes=62 * 1024 * 1024),
        cost_estimate=pl.CostEstimate(
            flops=6 * rows * hidden * local_width * nt,
            bytes_accessed=6 * hidden * local_width * nt, transcendentals=rows * hidden),
    )(tokens, meta, gate_weight, up_weight, down_weight)

def assign(flat, targets, capacity):
    hit = (flat[:, None, :] == targets[:, :, None]).astype(jnp.int32)
    rank = jnp.cumsum(hit, axis=2) - hit
    slots = lax.broadcasted_iota(jnp.int32, (1, 1, capacity, 1), 2)
    picked = (rank[:, :, None, :] == slots) & (hit[:, :, None, :] == 1)
    return picked.astype(jnp.float32)


def split_parts(values):
    upper = values.astype(jnp.bfloat16)
    lower = (values - upper.astype(jnp.float32)).astype(jnp.bfloat16)
    return (upper, lower)


def per_device(tokens, routes, route_weights, gate_weight, up_weight, down_weight):
    expert_count = lax.axis_size("expert")
    copies = expert_count // EXPERTS
    tok_count = tokens.shape[0]
    local_width = tokens.shape[1]
    features = lax.all_gather(tokens, "tensor", axis=1, tiled=True)
    width = features.shape[1]
    flat = routes.reshape(1, -1)
    targets = lax.broadcasted_iota(jnp.int32, (1, EXPERTS), 1)
    table = assign(flat, targets, CAP)[0]
    doubled = jnp.repeat(features, TOP, axis=0)
    packed = jnp.einsum(
        "ecq,qd->ecd", table.astype(jnp.bfloat16), doubled, preferred_element_type=jnp.float32
    ).astype(jnp.bfloat16)
    outgoing = jnp.broadcast_to(packed[:, None], (EXPERTS, copies, CAP, width)).reshape(
        expert_count, CAP, width
    )
    incoming = lax.all_to_all(outgoing, "expert", split_axis=0, concat_axis=0, tiled=True)
    received = incoming.reshape(expert_count * CAP, width)
    gate = jnp.dot(received, gate_weight, preferred_element_type=jnp.float32)
    up = jnp.dot(received, up_weight, preferred_element_type=jnp.float32)
    hidden = (jax.nn.silu(gate) * up).astype(jnp.bfloat16)
    partial_rows = lax.psum_scatter(
        lax.dot_general(
            down_weight, hidden, (((0,), (1,)), ((), ())), preferred_element_type=jnp.float32
        ).astype(jnp.bfloat16),
        "tensor",
        scatter_dimension=0,
        tiled=True,
    ).astype(jnp.float32)
    returned = lax.all_to_all(
        partial_rows.astype(jnp.bfloat16), "expert", split_axis=1, concat_axis=1, tiled=True
    ).astype(partial_rows.dtype)
    summed = (
        returned.reshape(local_width, EXPERTS, copies, CAP)
        .sum(axis=2)
        .reshape(local_width, EXPERTS * CAP)
    )
    selector = table.reshape(EXPERTS * CAP, -1).astype(jnp.bfloat16)
    upper, lower = split_parts(summed)
    gathered = jnp.dot(upper, selector, preferred_element_type=jnp.float32) + jnp.dot(
        lower, selector, preferred_element_type=jnp.float32
    )
    scales = route_weights.astype(jnp.float32).reshape(1, -1)
    result = (gathered * scales).reshape(local_width, tok_count, TOP).sum(axis=2)
    return result.T.astype(jnp.bfloat16)


def solution(mesh):
    in_specs = (
        P(("groups", "expert"), "tensor"),
        P(("groups", "expert"), None),
        P(("groups", "expert"), None),
        P(None, ("expert", "tensor")),
        P(None, ("expert", "tensor")),
        P(("expert", "tensor"), None),
    )
    out_specs = P(("groups", "expert"), "tensor")
    small = mesh.shape["expert"] == EXPERTS and mesh.shape["tensor"] > 1
    body = functools.partial(fused, mesh) if small else per_device
    return jax.shard_map(
        body, mesh=mesh, in_specs=in_specs, out_specs=out_specs, check_vma=False
    )
```

```python
import functools

import jax
import jax.numpy as jnp
from jax import lax
from jax.experimental import pallas as pl
from jax.experimental.pallas import tpu as pltpu
from jax.sharding import PartitionSpec as P

EXPERTS = 4
TOP = 2
CAP = 72
BF = jnp.bfloat16
F32 = jnp.float32
W_SLOTS = 3
D_SLOTS = 3
K_SLOTS = 6
FWD_LAG = 2
DOT_LAG = 3
X_LAG = 2
Z_LAG = 4
ROLES = 4


def kernel(
    nt, nq, tok, meta, wg, wu, wd, out,
    xbuf, packed, acc_g, acc_u, hid, gbuf, ubuf, dbuf, pick, spread, meta_in,
    keep, sib_out, sib_in, x_out, x_in, z_out, z_in,
    tok_sem, w_sem, d_sem, meta_s, meta_r,
    zs_s, zs_r, xs_s, xs_r, own_s, own_r, fwd_s, fwd_r,
    rsib_s, rsib_r, rx_s, rx_r, rz_s, rz_r,
):
    n = nt * nq
    kc = xbuf.shape[3]
    tokens = tok.shape[0]
    rows = ROLES * CAP
    z = lax.axis_index("tensor")
    ex = lax.axis_index("expert")
    core = lax.rem(ex, 2)
    chip = lax.div(ex, 2)
    sib = 2 * chip + 1 - core
    xp = 2 * (1 - chip) + core
    dg = 2 * (1 - chip) + 1 - core
    my_expert = ex

    def offset(d):
        return lax.rem(z + ((d + 1) // 2) * (2 * (d % 2) - 1) + nt, nt)

    def offset_t(d):
        return lax.rem(z + lax.div(d + 1, 2) * (2 * lax.rem(d, 2) - 1) + nt, nt)

    def at_expert(src, dst, s, r, who):
        return pltpu.make_async_remote_copy(
            src_ref=src, dst_ref=dst, send_sem=s, recv_sem=r,
            device_id={"expert": who}, device_id_type=pl.DeviceIdType.MESH)

    def at_tensor(src, dst, s, r, who):
        return pltpu.make_async_remote_copy(
            src_ref=src, dst_ref=dst, send_sem=s, recv_sem=r,
            device_id={"tensor": who}, device_id_type=pl.DeviceIdType.MESH)

    def tok_copy(q):
        return pltpu.make_async_copy(
            tok.at[:, pl.ds(q * kc, kc)], xbuf.at[z * nq + q, 0], tok_sem.at[q])

    def g_copy(i, k):
        s = lax.rem(i, W_SLOTS)
        r = pl.ds(pl.multiple_of(k * kc, kc), kc)
        return pltpu.make_async_copy(wg.at[r, :], gbuf.at[s], w_sem.at[0, s])

    def u_copy(i, k):
        s = lax.rem(i, W_SLOTS)
        r = pl.ds(pl.multiple_of(k * kc, kc), kc)
        return pltpu.make_async_copy(wu.at[r, :], ubuf.at[s], w_sem.at[1, s])

    def d_copy(i, k):
        s = lax.rem(i, D_SLOTS)
        r = pl.ds(pl.multiple_of(k * kc, kc), kc)
        return pltpu.make_async_copy(wd.at[:, r], dbuf.at[s], d_sem.at[s])

    def in_chunk(i):
        return offset_t(lax.rem(i, nt)) * nq + lax.div(i, nt)

    def out_owner(i):
        return offset_t(lax.rem(i + 1, nt))

    def out_chunk(i):
        return out_owner(i) * nq + lax.div(i, nt)

    def z_copy(d, q):
        s = (d - 1) * nq + q
        k = z * nq + q
        return at_tensor(xbuf.at[k, 0], xbuf.at[k, 0], zs_s.at[s], zs_r.at[k], offset(d))

    def z_arrival(k):
        return at_tensor(xbuf.at[k, 0], xbuf.at[k, 0], zs_s.at[0], zs_r.at[k], offset(1))

    def x_copy(k):
        return at_expert(xbuf.at[k, 0], xbuf.at[k, 1], xs_s.at[k], xs_r.at[k], xp)

    def own_copy(k):
        return at_expert(xbuf.at[k, 0], xbuf.at[k, 2], own_s.at[k], own_r.at[k], sib)

    def fwd_copy(k):
        return at_expert(xbuf.at[k, 1], xbuf.at[k, 3], fwd_s.at[k], fwd_r.at[k], sib)

    def rsib_copy(k):
        return at_expert(sib_out.at[k], sib_in.at[k], rsib_s.at[k], rsib_r.at[k], sib)

    def rx_copy(k):
        return at_expert(x_out.at[k], x_in.at[k], rx_s.at[k], rx_r.at[k], xp)

    def rz_copy(k, q, who):
        return at_tensor(z_out.at[k], z_in.at[z * nq + q], rz_s.at[k], rz_r.at[z * nq + q], who)

    def rz_arrival(k):
        return at_tensor(z_out.at[k], z_in.at[k], rz_s.at[k], rz_r.at[k], offset(1))

    def meta_copy(role, who):
        return at_expert(
            meta.at[who], meta_in.at[role], meta_s.at[role], meta_r.at[role], who)

    for q in range(nq):
        tok_copy(q).start()
    for i in range(W_SLOTS):
        g_copy(i, in_chunk(i)).start()
        u_copy(i, in_chunk(i)).start()

    barrier = pltpu.get_barrier_semaphore()
    for who in (sib, xp, dg):
        pl.semaphore_signal(
            barrier, inc=1, device_id={"expert": who}, device_id_type=pl.DeviceIdType.MESH)
    for d in range(1, nt):
        pl.semaphore_signal(
            barrier, inc=1, device_id={"tensor": offset(d)}, device_id_type=pl.DeviceIdType.MESH)
    pl.semaphore_wait(barrier, 3 + nt - 1)

    partners = ((1, xp), (2, sib), (3, dg))
    for role, who in partners:
        meta_copy(role, who).start()
    for q in range(nq):
        tok_copy(q).wait()
        for d in range(1, nt):
            z_copy(d, q).start()
        x_copy(z * nq + q).start()
        own_copy(z * nq + q).start()
    for i in range(D_SLOTS):
        d_copy(i, out_chunk(i)).start()

    acc_g[...] = jnp.zeros_like(acc_g)
    acc_u[...] = jnp.zeros_like(acc_u)
    meta_in[0] = meta[my_expert]
    for role, who in partners:
        meta_copy(role, who).wait_recv()
    eye = lax.broadcasted_iota(jnp.int32, (tokens, tokens), 0) == lax.broadcasted_iota(
        jnp.int32, (tokens, tokens), 1)
    row_id = lax.broadcasted_iota(jnp.int32, (rows, tokens), 0).astype(F32)
    for role in range(ROLES):
        slot = meta_in[role, 0:1, :]
        weight = meta_in[role, 1:2, :]
        slot = jnp.where(slot >= 0, slot + role * CAP, -1.0)
        hot = jnp.where(row_id == slot, 1.0, 0.0).astype(BF)
        pick[:, role * tokens:(role + 1) * tokens] = hot
        scale = jnp.where(eye, jnp.broadcast_to(weight, (tokens, tokens)), 0.0).astype(BF)
        spread[role * tokens:(role + 1) * tokens, :] = lax.dot_general(
            scale, hot, (((1,), (1,)), ((), ())), preferred_element_type=F32).astype(BF)

    tile = 512 if gbuf.shape[2] % 512 == 0 else gbuf.shape[2]

    def gather_step(i, carry):
        @pl.when(i < n)
        def _():
            @pl.when(lax.rem(i, nt) > 0)
            def _():
                k = in_chunk(i)
                z_arrival(k).wait_recv()
                x_copy(k).start()
                own_copy(k).start()

        @pl.when((i >= FWD_LAG) & (i < n + FWD_LAG))
        def _():
            k = in_chunk(i - FWD_LAG)
            x_copy(k).wait_recv()
            fwd_copy(k).start()

        @pl.when(i >= DOT_LAG)
        def _():
            j = i - DOT_LAG
            k = in_chunk(j)
            s = lax.rem(j, W_SLOTS)
            own_copy(k).wait_recv()
            fwd_copy(k).wait_recv()
            packed[...] = jnp.dot(
                pick[...], xbuf[k].reshape(ROLES * tokens, kc), preferred_element_type=F32
            ).astype(BF)
            g_copy(j, k).wait()
            u_copy(j, k).wait()

            def column(t, c2):
                cols = pl.ds(pl.multiple_of(t * tile, tile), tile)
                acc_g[:, cols] += jnp.dot(packed[...], gbuf[s, :, cols], preferred_element_type=F32)
                acc_u[:, cols] += jnp.dot(packed[...], ubuf[s, :, cols], preferred_element_type=F32)
                return c2

            lax.fori_loop(0, gbuf.shape[2] // tile, column, 0)

            @pl.when(j + W_SLOTS < n)
            def _():
                k2 = in_chunk(j + W_SLOTS)
                g_copy(j + W_SLOTS, k2).start()
                u_copy(j + W_SLOTS, k2).start()

        return carry

    lax.fori_loop(0, n + DOT_LAG, gather_step, 0)

    def activate(t, carry):
        cols = pl.ds(pl.multiple_of(t * tile, tile), tile)
        hid[:, cols] = (jax.nn.silu(acc_g[:, cols]) * acc_u[:, cols]).astype(BF)
        return carry

    lax.fori_loop(0, gbuf.shape[2] // tile, activate, 0)

    width = kc

    def return_step(i, carry):
        @pl.when(i < n)
        def _():
            k = out_chunk(i)
            s = lax.rem(i, D_SLOTS)
            ks = lax.rem(i, K_SLOTS)
            d_copy(i, k).wait()

            def column(t, c2):
                cols = pl.ds(pl.multiple_of(t * width, width), width)
                term = jnp.dot(hid[...], dbuf[s, :, cols], preferred_element_type=F32).astype(BF)
                share = jnp.dot(spread[...], term, preferred_element_type=F32)
                keep[ks, :, cols] = share[:2 * tokens]
                sib_out[k, :, cols] = share[2 * tokens:].astype(BF)
                return c2

            lax.fori_loop(0, kc // width, column, 0)
            rsib_copy(k).start()

            @pl.when(i + D_SLOTS < n)
            def _():
                d_copy(i + D_SLOTS, out_chunk(i + D_SLOTS)).start()

        @pl.when((i >= X_LAG) & (i < n + X_LAG))
        def _():
            k = out_chunk(i - X_LAG)
            ks = lax.rem(i - X_LAG, K_SLOTS)
            rsib_copy(k).wait_recv()
            x_out[k] = (keep[ks, tokens:] + sib_in[k, tokens:].astype(F32)).astype(BF)
            rx_copy(k).start()

        @pl.when(i >= Z_LAG)
        def _():
            j = i - Z_LAG
            k = out_chunk(j)
            ks = lax.rem(j, K_SLOTS)
            rx_copy(k).wait_recv()
            z_out[k] = (
                keep[ks, :tokens] + sib_in[k, :tokens].astype(F32) + x_in[k].astype(F32)
            ).astype(BF)

            @pl.when(lax.rem(j + 1, nt) > 0)
            def _():
                rz_copy(k, lax.div(j, nt), out_owner(j)).start()

        return carry

    lax.fori_loop(0, n + Z_LAG, return_step, 0)

    for q in range(nq):
        total = z_out[z * nq + q].astype(F32)
        for d in range(1, nt):
            k = offset(d) * nq + q
            rz_arrival(k).wait_recv()
            total = total + z_in[k].astype(F32)
        out[:, q * kc:(q + 1) * kc] = total.astype(BF)

    for role, who in partners:
        meta_copy(role, who).wait_send()
    for q in range(nq):
        for d in range(1, nt):
            z_copy(d, q).wait_send()

    def drain(k, carry):
        x_copy(k).wait_send()
        own_copy(k).wait_send()
        fwd_copy(k).wait_send()
        rsib_copy(k).wait_send()
        rx_copy(k).wait_send()
        return carry

    lax.fori_loop(0, n, drain, 0)
    for q in range(nq):
        for d in range(1, nt):
            rz_copy(offset(d) * nq + q, q, offset(d)).wait_send()


def fused(mesh, tokens, routes, route_weights, gate_weight, up_weight, down_weight):
    nt = mesh.shape["tensor"]
    count, local_width = tokens.shape
    hidden = gate_weight.shape[1]
    kc = 768
    nq = local_width // kc
    n = nt * nq
    rows = ROLES * CAP
    ids = lax.broadcasted_iota(jnp.int32, (EXPERTS, 1, 1), 0)
    named = routes.T[None] == ids
    hit = named.any(axis=1)
    share = jnp.where(named, route_weights.T.astype(F32)[None], 0.0).sum(axis=1)
    before = (
        lax.broadcasted_iota(jnp.int32, (count, count), 0)
        < lax.broadcasted_iota(jnp.int32, (count, count), 1)
    )
    rank = jnp.dot(hit.astype(BF), before.astype(BF), preferred_element_type=F32)
    slot = jnp.where(hit, rank, -1.0)
    meta = jnp.concatenate(
        [slot[:, None], share[:, None], jnp.zeros((EXPERTS, 6, count), F32)], axis=1)
    dma = pltpu.SemaphoreType.DMA
    vmem = pltpu.VMEM
    any_spec = pl.BlockSpec(memory_space=pl.ANY)
    vmem_spec = pl.BlockSpec(memory_space=pltpu.VMEM)
    return pl.pallas_call(
        functools.partial(kernel, nt, nq),
        out_shape=jax.ShapeDtypeStruct((count, local_width), BF),
        in_specs=[any_spec, vmem_spec, any_spec, any_spec, any_spec],
        out_specs=vmem_spec,
        scratch_shapes=[
            vmem((n, ROLES, count, kc), BF),
            vmem((rows, kc), BF),
            vmem((rows, hidden), F32),
            vmem((rows, hidden), F32),
            vmem((rows, hidden), BF),
            vmem((W_SLOTS, kc, hidden), BF),
            vmem((W_SLOTS, kc, hidden), BF),
            vmem((D_SLOTS, hidden, kc), BF),
            vmem((rows, ROLES * count), BF),
            vmem((ROLES * count, rows), BF),
            vmem((ROLES, 8, count), F32),
            vmem((K_SLOTS, 2 * count, kc), F32),
            vmem((n, 2 * count, kc), BF),
            vmem((n, 2 * count, kc), BF),
            vmem((n, count, kc), BF),
            vmem((n, count, kc), BF),
            vmem((n, count, kc), BF),
            vmem((n, count, kc), BF),
            dma((nq,)), dma((2, W_SLOTS)), dma((D_SLOTS,)), dma((ROLES,)), dma((ROLES,)),
            dma(((nt - 1) * nq,)), dma((n,)), dma((n,)), dma((n,)), dma((n,)), dma((n,)),
            dma((n,)), dma((n,)), dma((n,)), dma((n,)), dma((n,)), dma((n,)), dma((n,)), dma((n,)),
        ],
        compiler_params=pltpu.CompilerParams(
            collective_id=0, has_side_effects=True, vmem_limit_bytes=62 * 1024 * 1024),
        cost_estimate=pl.CostEstimate(
            flops=6 * rows * hidden * local_width * nt,
            bytes_accessed=6 * hidden * local_width * nt, transcendentals=rows * hidden),
    )(tokens, meta, gate_weight, up_weight, down_weight)

def assign(flat, targets, capacity):
    hit = (flat[:, None, :] == targets[:, :, None]).astype(jnp.int32)
    rank = jnp.cumsum(hit, axis=2) - hit
    slots = lax.broadcasted_iota(jnp.int32, (1, 1, capacity, 1), 2)
    picked = (rank[:, :, None, :] == slots) & (hit[:, :, None, :] == 1)
    return picked.astype(jnp.float32)


def split_parts(values):
    upper = values.astype(jnp.bfloat16)
    lower = (values - upper.astype(jnp.float32)).astype(jnp.bfloat16)
    return (upper, lower)


def per_device(tokens, routes, route_weights, gate_weight, up_weight, down_weight):
    expert_count = lax.axis_size("expert")
    copies = expert_count // EXPERTS
    tok_count = tokens.shape[0]
    local_width = tokens.shape[1]
    features = lax.all_gather(tokens, "tensor", axis=1, tiled=True)
    width = features.shape[1]
    flat = routes.reshape(1, -1)
    targets = lax.broadcasted_iota(jnp.int32, (1, EXPERTS), 1)
    table = assign(flat, targets, CAP)[0]
    doubled = jnp.repeat(features, TOP, axis=0)
    packed = jnp.einsum(
        "ecq,qd->ecd", table.astype(jnp.bfloat16), doubled, preferred_element_type=jnp.float32
    ).astype(jnp.bfloat16)
    outgoing = jnp.broadcast_to(packed[:, None], (EXPERTS, copies, CAP, width)).reshape(
        expert_count, CAP, width
    )
    incoming = lax.all_to_all(outgoing, "expert", split_axis=0, concat_axis=0, tiled=True)
    received = incoming.reshape(expert_count * CAP, width)
    gate = jnp.dot(received, gate_weight, preferred_element_type=jnp.float32)
    up = jnp.dot(received, up_weight, preferred_element_type=jnp.float32)
    hidden = (jax.nn.silu(gate) * up).astype(jnp.bfloat16)
    partial_rows = lax.psum_scatter(
        lax.dot_general(
            down_weight, hidden, (((0,), (1,)), ((), ())), preferred_element_type=jnp.float32
        ).astype(jnp.bfloat16),
        "tensor",
        scatter_dimension=0,
        tiled=True,
    ).astype(jnp.float32)
    returned = lax.all_to_all(
        partial_rows.astype(jnp.bfloat16), "expert", split_axis=1, concat_axis=1, tiled=True
    ).astype(partial_rows.dtype)
    summed = (
        returned.reshape(local_width, EXPERTS, copies, CAP)
        .sum(axis=2)
        .reshape(local_width, EXPERTS * CAP)
    )
    selector = table.reshape(EXPERTS * CAP, -1).astype(jnp.bfloat16)
    upper, lower = split_parts(summed)
    gathered = jnp.dot(upper, selector, preferred_element_type=jnp.float32) + jnp.dot(
        lower, selector, preferred_element_type=jnp.float32
    )
    scales = route_weights.astype(jnp.float32).reshape(1, -1)
    result = (gathered * scales).reshape(local_width, tok_count, TOP).sum(axis=2)
    return result.T.astype(jnp.bfloat16)


def solution(mesh):
    in_specs = (
        P(("groups", "expert"), "tensor"),
        P(("groups", "expert"), None),
        P(("groups", "expert"), None),
        P(None, ("expert", "tensor")),
        P(None, ("expert", "tensor")),
        P(("expert", "tensor"), None),
    )
    out_specs = P(("groups", "expert"), "tensor")
    small = mesh.shape["expert"] == EXPERTS and mesh.shape["tensor"] > 1
    body = functools.partial(fused, mesh) if small else per_device
    return jax.shard_map(
        body, mesh=mesh, in_specs=in_specs, out_specs=out_specs, check_vma=False
    )
```
